32 devices in a mesh: win: 2 (over x), sub: 16 (over z, y, core).
Axes of the slice: x: 2, y: 2, z: 4, core: 2. Of those that a mesh axis runs over, the one named last changes fastest.
Arguments:
- pulses: bfloat16 [32, 80, 2, 4096], P(('win', 'sub')), parts along dimension 0, may hold values from -6 to 6
- offsets: int32 [32, 80], P(('win', 'sub')), parts along dimension 0, may hold values from 0 to 3968
- geometry: float32 [32, 3, 80], P(('win', 'sub')), parts along dimension 0, may hold values from -1 to 1
- counts: int32 [32], P(('win', 'sub')), parts along dimension 0, may hold values from 48 to 80, as said below
Outputs:
- frames: float32 [32, 2, 32, 512], P(('win', 'sub')), parts along dimension 0
- cumulative: float32 [32, 2, 32, 512], P(('win', 'sub')), parts along dimension 0
The draws below stay inside these ranges and needn't reach their ends.
There are 2 independent parts, one for each index of `win`. The reference program is written for one: setup_inputs(seed, part) draws one part's arguments, and reference() takes and returns one part's arrays. A program takes and returns all parts, laid end to end along the dimension named above; each array names one. Nothing has to cross between parts.
Inputs may be any that keep to these rules, and one draw needn't show every extreme that they name: Subaperture s holds its pulses in slots 0 to counts[s] - 1; the other slots are unused. Some subaperture has 80 pulses and some 48.
All inputs are finite; a program needn't handle non-finite values.
Results may differ from the reference program's by a relative error of at most 0.004.
Values sent between devices are 32-bit elements; how exact they have to be, the bound alone decides.
No kernel may reach another device: no remote copies, remote signals or barrier semaphores. Data moves between devices by JAX's collectives and lax.ppermute only.
A program may use at most 192 MiB of HBM per device.

```python
import math
import jax
import jax.numpy as jnp
from jax import lax

ROWS = 32
COLS = 512
SAMPLES = 4096
BINS = 128
PULSES = 80
FEWEST = 48
SUBAPS = 16


def draw_counts(key, part):
    first_key, second_key = jax.random.split(jax.random.fold_in(key, 7071))
    base = jax.random.randint(first_key, (SUBAPS,), FEWEST, PULSES + 1, dtype=jnp.int32)
    order = jax.random.permutation(second_key, SUBAPS)
    base = base.at[order[0]].set(PULSES)
    base = base.at[order[1]].set(FEWEST)
    return base.astype(jnp.int32)


def touch_ends(entries, stream_key, low, top_value):
    index_at = [jax.random.randint(jax.random.fold_in(stream_key, axis), (), 0, length) for axis, length in enumerate(entries.shape)]
    main_axis = entries.shape.index(max(entries.shape))
    neighbour = index_at[:main_axis] + [(index_at[main_axis] + 1) % entries.shape[main_axis]] + index_at[main_axis + 1:]
    return entries.at[tuple(index_at)].set(low).at[tuple(neighbour)].set(top_value)


def shard_levels(stream_key, shape, pieces, smallest, high):
    level = 1.0
    for axis_at, blocks in pieces:
        heights = jax.random.uniform(jax.random.fold_in(jax.random.fold_in(stream_key, 6), axis_at), (blocks,), jnp.float32, smallest / len(pieces), high / len(pieces))
        level = level * jnp.repeat(jnp.exp(heights), shape[axis_at] // blocks).reshape((-1,) + (1,) * (len(shape) - 1 - axis_at))
    return level


def noise(key, extent, deviation, reach, pieces=(), held_as=jnp.bfloat16):
    drawn = deviation * jax.random.normal(key, extent, jnp.float32)
    if pieces:
        drawn = drawn * shard_levels(key, extent, pieces, -0.22, 0.18)
    return jnp.clip(drawn, -reach, reach).astype(held_as)


def setup_inputs(seed: int = 0, part: int = 0) -> dict:
    splits = jax.random.split(jax.random.key(seed), 5)
    own_keys = jax.random.split(jax.random.fold_in(splits[4], part), 5)
    return {
        "pulses": noise(own_keys[0], (SUBAPS, PULSES, 2, SAMPLES), 1.0, 6.0, ((0, 16),)),
        "offsets": touch_ends(jax.random.randint(own_keys[1], (SUBAPS, PULSES), 0, SAMPLES - BINS + 1), jax.random.fold_in(own_keys[1], 1), 0, SAMPLES - BINS).astype(jnp.int32),
        "geometry": jnp.clip(jax.random.uniform(own_keys[2], (SUBAPS, 3, PULSES), jnp.float32, -1.0, 1.0) * shard_levels(own_keys[2], (SUBAPS, 3, PULSES), ((0, 16),), -0.4, 0.0), -1.0, 1.0),
        "counts": draw_counts(jax.random.fold_in(jax.random.fold_in(splits[4], part), 71), part),
    }


def spectrum_of(pulse_rows, vertical_offset_along, geometry_sub, count, width):
    slots = pulse_rows.shape[0]
    windows = jax.vmap(lambda one_row, offset: lax.dynamic_slice_in_dim(one_row, offset, width, 1))(pulse_rows, vertical_offset_along.astype(jnp.int32)).astype(jnp.float32)
    index = jnp.arange(width, dtype=jnp.int32)
    shifted = index - width // 2
    turns = index[:, None] * shifted[None, :] % width
    angle = 2.0 * math.pi / width * turns.astype(jnp.float32)
    cosine = jnp.cos(angle)
    sine = jnp.sin(angle)
    highest = lax.Precision.HIGHEST
    real_in = windows[:, 0]
    imag_in = windows[:, 1]
    real_out = (jnp.dot(real_in, cosine, precision=highest) + jnp.dot(imag_in, sine, precision=highest)) / width
    imag_out = (jnp.dot(imag_in, cosine, precision=highest) - jnp.dot(real_in, sine, precision=highest)) / width
    viewing_bearing = 2.0 * math.pi * (shifted.astype(jnp.float32) / width + 0.37)
    scene_middle = width / 2.0 + width / 16.0 * geometry_sub[0]
    radar_frequency = 2.0 * math.pi / 100.0 * (37 * vertical_offset_along % 100).astype(jnp.float32)
    signal_argument = viewing_bearing[None, :] * scene_middle[:, None] + radar_frequency[:, None]
    live = (jnp.arange(slots, dtype=jnp.int32) < count).astype(jnp.float32) / math.sqrt(slots)
    cos_phase = jnp.cos(signal_argument)
    sin_phase = jnp.sin(signal_argument)
    coefficient_real = live[:, None] * (real_out * cos_phase - imag_out * sin_phase)
    coef_im = live[:, None] * (real_out * sin_phase + imag_out * cos_phase)
    return (coefficient_real, coef_im, viewing_bearing)

def block_product(coefficient_real, coef_im, viewing_bearing, row_slope, column_gradient, rows, cols):
    xpos = (jnp.arange(rows, dtype=jnp.int32) - rows // 2).astype(jnp.float32)
    ypos = (jnp.arange(cols, dtype=jnp.int32) - cols // 2).astype(jnp.float32)
    angle_x = xpos[:, None, None] * (viewing_bearing[None, :] * row_slope[:, None])[None]
    cosine_x = jnp.cos(angle_x)
    sine_x = jnp.sin(angle_x)
    left_re = coefficient_real[None] * cosine_x - coef_im[None] * sine_x
    left_im = coefficient_real[None] * sine_x + coef_im[None] * cosine_x
    left = jnp.concatenate([left_re.reshape(rows, -1), left_im.reshape(rows, -1)], axis=1).astype(jnp.bfloat16)
    angle_y = (viewing_bearing[None, :] * column_gradient[:, None])[:, :, None] * ypos[None, None, :]
    right_re = jnp.cos(angle_y).reshape(-1, cols)
    right_im = jnp.sin(angle_y).reshape(-1, cols)
    upper = jnp.concatenate([right_re, right_im], axis=1)
    lower = jnp.concatenate([-right_im, right_re], axis=1)
    right = jnp.concatenate([upper, lower], axis=0).astype(jnp.bfloat16)
    return jnp.dot(left, right, preferred_element_type=jnp.float32)

def single_picture(pulse_rows, vertical_offset_along, geometry_sub, count):
    coefficient_real, coef_im, viewing_bearing = spectrum_of(pulse_rows, vertical_offset_along, geometry_sub, count, BINS)
    row_slope = 0.05 * geometry_sub[1]
    column_gradient = 0.05 * geometry_sub[2]

    def add_block(step, total):
        start = (step * 8).astype(jnp.int32)
        part_re = lax.dynamic_slice_in_dim(coefficient_real, start, 8, 0)
        part_im = lax.dynamic_slice_in_dim(coef_im, start, 8, 0)
        slope_r = lax.dynamic_slice_in_dim(row_slope, start, 8, 0)
        slope_c = lax.dynamic_slice_in_dim(column_gradient, start, 8, 0)
        return total + block_product(part_re, part_im, viewing_bearing, slope_r, slope_c, ROWS, COLS)
    total = lax.fori_loop(0, PULSES // 8, add_block, jnp.zeros((ROWS, 2 * COLS), jnp.float32))
    return jnp.stack([total[:, :COLS], total[:, COLS:]], axis=0)

def reference(pulses, offsets, geometry, counts):
    image_frames = lax.map(lambda items: single_picture(items[0], items[1], items[2], items[3]), (pulses, offsets, geometry, counts))
    prefix = jnp.cumsum(image_frames, axis=0)
    lagged = jnp.concatenate([jnp.zeros((8,) + prefix.shape[1:], jnp.float32), prefix[:-8]], axis=0)
    frames = (prefix - lagged) / math.sqrt(8.0)
    scale = jnp.sqrt(jnp.arange(1, SUBAPS + 1, dtype=jnp.int32).astype(jnp.float32))
    cumulative = prefix / scale[:, None, None, None]
    return (frames, cumulative)
```

```python
import functools
import math

import jax
import jax.numpy as jnp
from jax import lax
from jax.experimental import pallas as pl
from jax.experimental.pallas import tpu as pltpu
from jax.sharding import PartitionSpec as P

ROWS = 32
COLS = 512
BINS = 128
WINDOW = 8
LANES = 128
GROUP = 8

SIN = (3.141592580044369, -5.167706878903419, 2.5500313768938527, -0.5980451717629565, 0.07722012423151481)
COS = (0.999999953468687, -4.934792858755703, 4.0584119149345526, -1.3318801632613946, 0.21969679848706386)


def horner(coefficients, u):
    total = jnp.full_like(u, coefficients[-1])
    for c in coefficients[-2::-1]:
        total = total * u + c
    return total


def cis_turns(turns):
    f = turns - jnp.round(turns)
    u = f * f
    s = f * horner(SIN, u)
    c = horner(COS, u)
    return 1.0 - 2.0 * s * s, 2.0 * s * c


def cmul(a, b):
    return a[0] * b[0] - a[1] * b[1], a[0] * b[1] + a[1] * b[0]


def csquare(a):
    return a[0] * a[0] - a[1] * a[1], 2.0 * a[0] * a[1]


def image_kernel(rows, cols, width, counts_s, offsets_s, offsets_v, geometry_v, pulses_any, out_ref,
                 held, window_f32, columns, seeds, steps, acc, sem):
    slots, _, samples = held.shape
    pieces = cols // LANES
    load = pltpu.make_async_copy(pulses_any.at[0], held, sem)
    load.start()

    columns[...] = jnp.zeros_like(columns)
    columns[0:3, 0:slots] = geometry_v[0]
    columns[3:4, 0:slots] = offsets_v[...].astype(jnp.float32)
    by_pulse = jnp.transpose(columns[...])[0:slots]
    geo_centre = by_pulse[:, 0:1]
    slope_r = 0.05 * by_pulse[:, 1:2]
    slope_c = 0.05 * by_pulse[:, 2:3]
    offset = by_pulse[:, 3:4]
    shape = (slots, LANES)
    lane = lax.broadcasted_iota(jnp.int32, shape, 1).astype(jnp.float32)
    g = lane - width // 2
    theta = g / width + 0.37
    y_local = lane
    last_block = samples // LANES - 2
    block = jnp.minimum(jnp.floor(offset / LANES), last_block)
    rest = offset - LANES * block

    angle = slope_c * y_local
    base = cis_turns(angle * (0.37 - (width // 2) / width))
    one = cis_turns(angle / width)
    now = base
    for r in range(8):
        for k in range(2):
            seeds[2 + k, pl.ds(r, slots, stride=8), :] = now[k]
        if r < 7:
            now = cmul(now, one)
    ratio = csquare(csquare(csquare(one)))
    for level in range(4):
        for k in range(2):
            steps[8 + 2 * level + k] = ratio[k]
        ratio = csquare(ratio)

    row_one = cis_turns(theta * slope_r)
    ratio = csquare(csquare(csquare(row_one)))
    piece = cis_turns(theta * (slope_c * LANES))
    for level, value in enumerate((ratio, csquare(ratio), piece, csquare(piece))):
        for k in range(2):
            steps[2 * level + k] = value[k]

    b_index = lax.broadcasted_iota(jnp.int32, (width, width), 0).astype(jnp.float32)
    g_index = lax.broadcasted_iota(jnp.int32, (width, width), 1).astype(jnp.float32) - width // 2
    cosine, sine = cis_turns(b_index * g_index / width)
    fourier = jnp.concatenate(
        [jnp.concatenate([cosine, -sine], axis=1), jnp.concatenate([sine, cosine], axis=1)], axis=0
    )
    fourier_high = fourier.astype(jnp.bfloat16)
    fourier_low = (fourier - fourier_high.astype(jnp.float32)).astype(jnp.bfloat16)

    phase = theta * ((width / 2.0 + width / 16.0 * geo_centre) - slope_r * (rows // 2) - slope_c * (cols // 2))
    scaled = 37.0 * offset
    steps37 = (scaled - 100.0 * jnp.round(scaled / 100.0)) / 100.0
    circular = g * rest / width
    phase = phase + (circular - jnp.round(circular)) + steps37
    phase_cis = cis_turns(phase)

    load.wait()
    for p in range(slots):
        start = jnp.minimum(offsets_s[0, p] // LANES, last_block) * LANES
        pair = held[p, :, pl.ds(pl.multiple_of(start, LANES), 2 * LANES)].astype(jnp.float32)
        for half in range(2):
            window_f32[half, 2 * p:2 * p + 2, :] = pair[:, half * LANES:(half + 1) * LANES]
    in_first = lane >= rest
    parts = []
    for k in range(2):
        first = window_f32[0, pl.ds(k, slots, stride=2), :]
        second = window_f32[1, pl.ds(k, slots, stride=2), :]
        parts.append(jnp.where(in_first, first, second))
    folded = jnp.concatenate(parts, axis=1).astype(jnp.bfloat16)
    spectrum = jnp.dot(folded, fourier_high, preferred_element_type=jnp.float32) + jnp.dot(
        folded, fourier_low, preferred_element_type=jnp.float32
    )
    live = lax.broadcasted_iota(jnp.int32, shape, 0) < counts_s[0]
    scale = jnp.where(live, 1.0 / (width * math.sqrt(slots)), 0.0)
    now = cmul((spectrum[:, 0:LANES] * scale, spectrum[:, LANES:] * scale), phase_cis)
    for r in range(8):
        for k in range(2):
            seeds[k, pl.ds(r, slots, stride=8), :] = now[k]
        if r < 7:
            now = cmul(now, row_one)

    acc[...] = jnp.zeros_like(acc)

    def grown(seed, first_step, pulse):
        values = [seed]
        for level in range(4):
            step = tuple(
                jnp.broadcast_to(steps[first_step + 2 * level + k, pl.ds(pulse, 1), :], (8, LANES)) for k in range(2)
            )
            values = values + [cmul(v, step) for v in values]
        return [jnp.concatenate([v[k] for v in values], axis=0) for k in range(2)]

    def add_group(step, carry):
        lefts = []
        rights = []
        for i in range(GROUP):
            pulse = step * GROUP + i
            at = pl.ds(pl.multiple_of(8 * pulse, 8), 8)
            left = grown((seeds[0, at, :], seeds[1, at, :]), 0, pulse)
            lefts += [v.astype(jnp.bfloat16) for v in left]
            right_re, right_im = grown((seeds[2, at, :], seeds[3, at, :]), 8, pulse)
            rights.append(jnp.concatenate([right_re, right_im], axis=1).astype(jnp.bfloat16))
            rights.append(jnp.concatenate([-right_im, right_re], axis=1).astype(jnp.bfloat16))
        acc[...] += jnp.dot(
            jnp.concatenate(lefts, axis=1), jnp.concatenate(rights, axis=0), preferred_element_type=jnp.float32
        )
        return carry

    lax.fori_loop(0, slots // GROUP, add_group, 0)
    for piece_at in range(pieces):
        for k in range(2):
            out_ref[0, k, :, piece_at * LANES:(piece_at + 1) * LANES] = acc[
                piece_at * rows:(piece_at + 1) * rows, k * LANES:(k + 1) * LANES
            ]


def image_of(pulses, offsets, geometry, counts):
    _, slots, _, samples = pulses.shape
    vmem = pl.BlockSpec(memory_space=pltpu.VMEM)
    smem = pl.BlockSpec(memory_space=pltpu.SMEM)
    return pl.pallas_call(
        functools.partial(image_kernel, ROWS, COLS, BINS),
        out_shape=jax.ShapeDtypeStruct((1, 2, ROWS, COLS), jnp.float32),
        in_specs=[smem, smem, vmem, vmem, pl.BlockSpec(memory_space=pl.ANY)],
        out_specs=vmem,
        scratch_shapes=[
            pltpu.VMEM((slots, 2, samples), pulses.dtype),
            pltpu.VMEM((2, 2 * slots, LANES), jnp.float32),
            pltpu.VMEM((LANES, LANES), jnp.float32),
            pltpu.VMEM((4, 8 * slots, LANES), jnp.float32),
            pltpu.VMEM((16, slots, LANES), jnp.float32),
            pltpu.VMEM((COLS // LANES * ROWS, 2 * LANES), jnp.float32),
            pltpu.SemaphoreType.DMA(()),
        ],
        compiler_params=pltpu.CompilerParams(vmem_limit_bytes=40 * 1024 * 1024),
    )(counts, offsets, offsets, geometry, pulses)


def shards(pulses, offsets, geometry, counts):
    image = image_of(pulses, offsets, geometry, counts)
    members = lax.axis_size("sub")
    me = lax.axis_index("sub")
    position = me % WINDOW

    def exchange(value, distance):
        return lax.ppermute(value, "sub", [(i, i ^ distance) for i in range(members)])

    upto = image
    after = jnp.zeros_like(image)
    distance = 1
    while distance < min(WINDOW, members):
        other = exchange(upto + after, distance)
        upper = (me & distance) != 0
        upto = jnp.where(upper, upto + other, upto)
        after = jnp.where(upper, after, after + other)
        distance *= 2
    total = upto + after
    lagged = lax.ppermute(after, "sub", [(i, i + WINDOW) for i in range(members - WINDOW)])
    prefix = upto
    while distance < members:
        other = exchange(total, distance)
        upper = (me & distance) != 0
        prefix = jnp.where(upper, prefix + other, prefix)
        total = total + other
        distance *= 2
    frames = (upto + lagged) * (1.0 / math.sqrt(WINDOW))
    cumulative = prefix / jnp.sqrt((me + 1).astype(jnp.float32))
    return frames, cumulative


def solution(mesh):
    return jax.shard_map(
        shards,
        mesh=mesh,
        in_specs=(
            P(("win", "sub"), None, None, None),
            P(("win", "sub"), None),
            P(("win", "sub"), None, None),
            P(("win", "sub")),
        ),
        out_specs=(P(("win", "sub"), None, None, None), P(("win", "sub"), None, None, None)),
        check_vma=False,
    )
```

```python
import functools
import math

import jax
import jax.numpy as jnp
from jax import lax
from jax.experimental import pallas as pl
from jax.experimental.pallas import tpu as pltpu
from jax.sharding import PartitionSpec as P

ROWS = 32
COLS = 512
BINS = 128
WINDOW = 8
LANES = 128
GROUP = 8

SIN = (3.141592580044369, -5.167706878903419, 2.5500313768938527, -0.5980451717629565, 0.07722012423151481)
COS = (0.999999953468687, -4.934792858755703, 4.0584119149345526, -1.3318801632613946, 0.21969679848706386)


def horner(coefficients, u):
    total = jnp.full_like(u, coefficients[-1])
    for c in coefficients[-2::-1]:
        total = total * u + c
    return total


def cis_turns(turns):
    f = turns - jnp.round(turns)
    u = f * f
    s = f * horner(SIN, u)
    c = horner(COS, u)
    return 1.0 - 2.0 * s * s, 2.0 * s * c


def cmul(a, b):
    return a[0] * b[0] - a[1] * b[1], a[0] * b[1] + a[1] * b[0]


def csquare(a):
    return a[0] * a[0] - a[1] * a[1], 2.0 * a[0] * a[1]


def image_kernel(rows, cols, width, counts_s, offsets_s, offsets_v, geometry_v, pulses_any, kept_ref, sent_ref,
                 held, window_f32, columns, seeds, steps, acc, sem):
    slots, _, samples = held.shape
    pieces = cols // LANES
    load = pltpu.make_async_copy(pulses_any.at[0], held, sem)
    load.start()

    columns[...] = jnp.zeros_like(columns)
    columns[0:3, 0:slots] = geometry_v[0]
    columns[3:4, 0:slots] = offsets_v[...].astype(jnp.float32)
    by_pulse = jnp.transpose(columns[...])[0:slots]
    geo_centre = by_pulse[:, 0:1]
    slope_r = 0.05 * by_pulse[:, 1:2]
    slope_c = 0.05 * by_pulse[:, 2:3]
    offset = by_pulse[:, 3:4]
    shape = (slots, LANES)
    lane = lax.broadcasted_iota(jnp.int32, shape, 1).astype(jnp.float32)
    g = lane - width // 2
    theta = g / width + 0.37
    y_local = lane
    last_block = samples // LANES - 2
    block = jnp.minimum(jnp.floor(offset / LANES), last_block)
    rest = offset - LANES * block

    angle = slope_c * y_local
    base = cis_turns(angle * (0.37 - (width // 2) / width))
    one = cis_turns(angle / width)
    now = base
    for r in range(8):
        for k in range(2):
            seeds[2 + k, pl.ds(r, slots, stride=8), :] = now[k]
        if r < 7:
            now = cmul(now, one)
    ratio = csquare(csquare(csquare(one)))
    for level in range(4):
        for k in range(2):
            steps[8 + 2 * level + k] = ratio[k]
        ratio = csquare(ratio)

    row_one = cis_turns(theta * slope_r)
    ratio = csquare(csquare(csquare(row_one)))
    piece = cis_turns(theta * (slope_c * LANES))
    for level, value in enumerate((ratio, csquare(ratio), piece, csquare(piece))):
        for k in range(2):
            steps[2 * level + k] = value[k]

    b_index = lax.broadcasted_iota(jnp.int32, (width, width), 0).astype(jnp.float32)
    g_index = lax.broadcasted_iota(jnp.int32, (width, width), 1).astype(jnp.float32) - width // 2
    cosine, sine = cis_turns(b_index * g_index / width)
    fourier = jnp.concatenate(
        [jnp.concatenate([cosine, -sine], axis=1), jnp.concatenate([sine, cosine], axis=1)], axis=0
    )
    fourier_high = fourier.astype(jnp.bfloat16)
    fourier_low = (fourier - fourier_high.astype(jnp.float32)).astype(jnp.bfloat16)

    phase = theta * ((width / 2.0 + width / 16.0 * geo_centre) - slope_r * (rows // 2) - slope_c * (cols // 2))
    scaled = 37.0 * offset
    steps37 = (scaled - 100.0 * jnp.round(scaled / 100.0)) / 100.0
    circular = g * rest / width
    phase = phase + (circular - jnp.round(circular)) + steps37
    phase_cis = cis_turns(phase)

    load.wait()
    for p in range(slots):
        start = jnp.minimum(offsets_s[0, p] // LANES, last_block) * LANES
        pair = held[p, :, pl.ds(pl.multiple_of(start, LANES), 2 * LANES)].astype(jnp.float32)
        for half in range(2):
            window_f32[half, 2 * p:2 * p + 2, :] = pair[:, half * LANES:(half + 1) * LANES]
    in_first = lane >= rest
    parts = []
    for k in range(2):
        first = window_f32[0, pl.ds(k, slots, stride=2), :]
        second = window_f32[1, pl.ds(k, slots, stride=2), :]
        parts.append(jnp.where(in_first, first, second))
    folded = jnp.concatenate(parts, axis=1).astype(jnp.bfloat16)
    spectrum = jnp.dot(folded, fourier_high, preferred_element_type=jnp.float32) + jnp.dot(
        folded, fourier_low, preferred_element_type=jnp.float32
    )
    live = lax.broadcasted_iota(jnp.int32, shape, 0) < counts_s[0]
    scale = jnp.where(live, 1.0 / (width * math.sqrt(slots)), 0.0)
    now = cmul((spectrum[:, 0:LANES] * scale, spectrum[:, LANES:] * scale), phase_cis)
    for r in range(8):
        for k in range(2):
            seeds[k, pl.ds(r, slots, stride=8), :] = now[k]
        if r < 7:
            now = cmul(now, row_one)

    acc[...] = jnp.zeros_like(acc)

    def grown(seed, first_step, pulse):
        values = [seed]
        for level in range(4):
            step = tuple(
                jnp.broadcast_to(steps[first_step + 2 * level + k, pl.ds(pulse, 1), :], (8, LANES)) for k in range(2)
            )
            values = values + [cmul(v, step) for v in values]
        return [jnp.concatenate([v[k] for v in values], axis=0) for k in range(2)]

    def add_group(step, carry):
        lefts = []
        rights = []
        for i in range(GROUP):
            pulse = step * GROUP + i
            at = pl.ds(pl.multiple_of(8 * pulse, 8), 8)
            left = grown((seeds[0, at, :], seeds[1, at, :]), 0, pulse)
            lefts += [v.astype(jnp.bfloat16) for v in left]
            right_re, right_im = grown((seeds[2, at, :], seeds[3, at, :]), 8, pulse)
            rights.append(jnp.concatenate([right_re, right_im], axis=1).astype(jnp.bfloat16))
            rights.append(jnp.concatenate([-right_im, right_re], axis=1).astype(jnp.bfloat16))
        acc[...] += jnp.dot(
            jnp.concatenate(lefts, axis=1), jnp.concatenate(rights, axis=0), preferred_element_type=jnp.float32
        )
        return carry

    lax.fori_loop(0, slots // GROUP, add_group, 0)
    second = lax.rem(lax.axis_index("sub"), 2) == 1
    for piece_at in range(pieces):
        at = slice(piece_at * rows, (piece_at + 1) * rows)
        real, imag = acc[at, 0:LANES], acc[at, LANES:2 * LANES]
        lanes = slice(piece_at * LANES, (piece_at + 1) * LANES)
        kept_ref[:, lanes] = jnp.where(second, imag, real)
        sent_ref[:, lanes] = jnp.where(second, real, imag)


def halves_of_image(pulses, offsets, geometry, counts):
    _, slots, _, samples = pulses.shape
    vmem = pl.BlockSpec(memory_space=pltpu.VMEM)
    smem = pl.BlockSpec(memory_space=pltpu.SMEM)
    return pl.pallas_call(
        functools.partial(image_kernel, ROWS, COLS, BINS),
        out_shape=[jax.ShapeDtypeStruct((ROWS, COLS), jnp.float32)] * 2,
        in_specs=[smem, smem, vmem, vmem, pl.BlockSpec(memory_space=pl.ANY)],
        out_specs=[vmem, vmem],
        scratch_shapes=[
            pltpu.VMEM((slots, 2, samples), pulses.dtype),
            pltpu.VMEM((2, 2 * slots, LANES), jnp.float32),
            pltpu.VMEM((LANES, LANES), jnp.float32),
            pltpu.VMEM((4, 8 * slots, LANES), jnp.float32),
            pltpu.VMEM((16, slots, LANES), jnp.float32),
            pltpu.VMEM((COLS // LANES * ROWS, 2 * LANES), jnp.float32),
            pltpu.SemaphoreType.DMA(()),
        ],
        compiler_params=pltpu.CompilerParams(vmem_limit_bytes=40 * 1024 * 1024),
    )(counts, offsets, offsets, geometry, pulses)


def shards(pulses, offsets, geometry, counts):
    members = lax.axis_size("sub")
    me = lax.axis_index("sub")
    kept, sent = halves_of_image(pulses, offsets, geometry, counts)

    def swap(value, distance):
        return lax.ppermute(value, "sub", [(i, i ^ distance) for i in range(members)])

    def ahead(value, distance):
        return lax.ppermute(value, "sub", [(i, i + distance) for i in range(members - distance)])

    odd = me % 2 == 1
    upper = me // 2 % 2 == 1
    block = me // 4
    blocks = members // 4
    got = swap(sent, 1)
    first = jnp.where(odd, got, kept)
    second = jnp.where(odd, kept, got)
    pair = first + second

    if blocks <= 4:
        nothing = jnp.zeros_like(pair)
        earlier = last = before_last = oldest = nothing
        for k in range(1, blocks):
            value = jnp.stack([pair, second]) if k == 2 else pair
            value = swap(value, 4 * k)
            if k == 2:
                oldest = jnp.where(block >= 2, value[1], nothing)
                value = value[0]
                before_last = jnp.where(block >= 2, value, nothing)
            source = block ^ k
            earlier = earlier + jnp.where(source < block, value, nothing)
            last = last + jnp.where(source == block - 1, value, nothing)
    else:
        last = ahead(pair, 4)
        before_last, oldest = ahead(jnp.stack([pair, second]), 8)
        earlier = last
        distance = 4
        while distance < members:
            earlier = earlier + ahead(earlier, distance)
            distance *= 2

    mine = jnp.stack([
        earlier + jnp.where(upper, 0.0, pair),
        last + jnp.where(upper, before_last, pair),
    ])
    other = swap(mine, 2)
    earlier = earlier + other[0]
    recent = last + other[1]
    frame_scale = 1.0 / math.sqrt(WINDOW)
    number = (me - me % 2 + 1).astype(jnp.float32)
    firsts = jnp.stack([(first + recent + oldest) * frame_scale, (earlier + first) / jnp.sqrt(number)])
    seconds = jnp.stack([(pair + recent) * frame_scale, (earlier + pair) / jnp.sqrt(number + 1.0)])

    own = jnp.where(odd, seconds, firsts)
    back = swap(jnp.where(odd, firsts, seconds), 1)
    real = jnp.where(odd, back, own)
    imag = jnp.where(odd, own, back)
    frames, cumulative = jnp.stack([real, imag], axis=1)
    return frames[None], cumulative[None]


def solution(mesh):
    return jax.shard_map(
        shards,
        mesh=mesh,
        in_specs=(
            P(("win", "sub"), None, None, None),
            P(("win", "sub"), None),
            P(("win", "sub"), None, None),
            P(("win", "sub")),
        ),
        out_specs=(P(("win", "sub"), None, None, None), P(("win", "sub"), None, None, None)),
        check_vma=False,
    )
```

```python
import functools
import math

import jax
import jax.numpy as jnp
from jax import lax
from jax.experimental import pallas as pl
from jax.experimental.pallas import tpu as pltpu
from jax.sharding import PartitionSpec as P

ROWS = 32
COLS = 512
BINS = 128
WINDOW = 8
LANES = 128
GROUP = 8

SIN = (3.141592580044369, -5.167706878903419, 2.5500313768938527, -0.5980451717629565, 0.07722012423151481)
COS = (0.999999953468687, -4.934792858755703, 4.0584119149345526, -1.3318801632613946, 0.21969679848706386)


def horner(coefficients, u):
    total = jnp.full_like(u, coefficients[-1])
    for c in coefficients[-2::-1]:
        total = total * u + c
    return total


def cis_turns(turns):
    f = turns - jnp.round(turns)
    u = f * f
    s = f * horner(SIN, u)
    c = horner(COS, u)
    return 1.0 - 2.0 * s * s, 2.0 * s * c


def cmul(a, b):
    return a[0] * b[0] - a[1] * b[1], a[0] * b[1] + a[1] * b[0]


def csquare(a):
    return a[0] * a[0] - a[1] * a[1], 2.0 * a[0] * a[1]


def image_kernel(rows, cols, width, counts_s, offsets_h, geometry_h, pulses_h, kept_ref, sent_ref,
                 held, window_f32, geometry_v, offsets_v, offsets_s, columns, seeds, steps, acc, sems):
    slots, _, samples = held.shape
    pieces = cols // LANES
    small = [
        pltpu.make_async_copy(source, target, sems.at[k])
        for k, (source, target) in enumerate((
            (geometry_h, geometry_v), (offsets_h, offsets_v), (offsets_h, offsets_s),
        ))
    ]
    for copy in small:
        copy.start()
    load = pltpu.make_async_copy(pulses_h.at[0], held, sems.at[3])
    load.start()

    b_index = lax.broadcasted_iota(jnp.int32, (width, width), 0).astype(jnp.float32)
    g_index = lax.broadcasted_iota(jnp.int32, (width, width), 1).astype(jnp.float32) - width // 2
    cosine, sine = cis_turns(b_index * g_index / width)
    fourier = jnp.concatenate(
        [jnp.concatenate([cosine, -sine], axis=1), jnp.concatenate([sine, cosine], axis=1)], axis=0
    )
    fourier_high = fourier.astype(jnp.bfloat16)
    fourier_low = (fourier - fourier_high.astype(jnp.float32)).astype(jnp.bfloat16)

    columns[...] = jnp.zeros_like(columns)
    for copy in small:
        copy.wait()
    for k in range(3):
        columns[k:k + 1, 0:slots] = geometry_v[k]
    columns[3:4, 0:slots] = offsets_v[...].astype(jnp.float32)
    by_pulse = jnp.transpose(columns[...])[0:slots]
    geo_centre = by_pulse[:, 0:1]
    slope_r = 0.05 * by_pulse[:, 1:2]
    slope_c = 0.05 * by_pulse[:, 2:3]
    offset = by_pulse[:, 3:4]
    shape = (slots, LANES)
    lane = lax.broadcasted_iota(jnp.int32, shape, 1).astype(jnp.float32)
    g = lane - width // 2
    theta = g / width + 0.37
    y_local = lane
    last_block = samples // LANES - 2
    block = jnp.minimum(jnp.floor(offset / LANES), last_block)
    rest = offset - LANES * block

    angle = slope_c * y_local
    base = cis_turns(angle * (0.37 - (width // 2) / width))
    one = cis_turns(angle / width)
    now = base
    for r in range(8):
        for k in range(2):
            seeds[2 + k, pl.ds(r, slots, stride=8), :] = now[k]
        if r < 7:
            now = cmul(now, one)
    ratio = csquare(csquare(csquare(one)))
    for level in range(4):
        for k in range(2):
            steps[8 + 2 * level + k] = ratio[k]
        ratio = csquare(ratio)

    row_one = cis_turns(theta * slope_r)
    ratio = csquare(csquare(csquare(row_one)))
    piece = cis_turns(theta * (slope_c * LANES))
    for level, value in enumerate((ratio, csquare(ratio), piece, csquare(piece))):
        for k in range(2):
            steps[2 * level + k] = value[k]

    phase = theta * ((width / 2.0 + width / 16.0 * geo_centre) - slope_r * (rows // 2) - slope_c * (cols // 2))
    scaled = 37.0 * offset
    steps37 = (scaled - 100.0 * jnp.round(scaled / 100.0)) / 100.0
    circular = g * rest / width
    phase = phase + (circular - jnp.round(circular)) + steps37
    phase_cis = cis_turns(phase)

    load.wait()
    for p in range(slots):
        start = jnp.minimum(offsets_s[0, p] // LANES, last_block) * LANES
        pair = held[p, :, pl.ds(pl.multiple_of(start, LANES), 2 * LANES)].astype(jnp.float32)
        for half in range(2):
            window_f32[half, 2 * p:2 * p + 2, :] = pair[:, half * LANES:(half + 1) * LANES]
    in_first = lane >= rest
    parts = []
    for k in range(2):
        first = window_f32[0, pl.ds(k, slots, stride=2), :]
        second = window_f32[1, pl.ds(k, slots, stride=2), :]
        parts.append(jnp.where(in_first, first, second))
    folded = jnp.concatenate(parts, axis=1).astype(jnp.bfloat16)
    spectrum = jnp.dot(folded, fourier_high, preferred_element_type=jnp.float32) + jnp.dot(
        folded, fourier_low, preferred_element_type=jnp.float32
    )
    live = lax.broadcasted_iota(jnp.int32, shape, 0) < counts_s[0]
    scale = jnp.where(live, 1.0 / (width * math.sqrt(slots)), 0.0)
    now = cmul((spectrum[:, 0:LANES] * scale, spectrum[:, LANES:] * scale), phase_cis)
    for r in range(8):
        for k in range(2):
            seeds[k, pl.ds(r, slots, stride=8), :] = now[k]
        if r < 7:
            now = cmul(now, row_one)

    acc[...] = jnp.zeros_like(acc)

    def grown(seed, first_step, pulse):
        values = [seed]
        for level in range(4):
            step = tuple(
                jnp.broadcast_to(steps[first_step + 2 * level + k, pl.ds(pulse, 1), :], (8, LANES)) for k in range(2)
            )
            values = values + [cmul(v, step) for v in values]
        return [jnp.concatenate([v[k] for v in values], axis=0) for k in range(2)]

    def add_group(step, carry):
        lefts = []
        rights = []
        for i in range(GROUP):
            pulse = step * GROUP + i
            at = pl.ds(pl.multiple_of(8 * pulse, 8), 8)
            left = grown((seeds[0, at, :], seeds[1, at, :]), 0, pulse)
            lefts += [v.astype(jnp.bfloat16) for v in left]
            right_re, right_im = grown((seeds[2, at, :], seeds[3, at, :]), 8, pulse)
            rights.append(jnp.concatenate([right_re, right_im], axis=1).astype(jnp.bfloat16))
            rights.append(jnp.concatenate([-right_im, right_re], axis=1).astype(jnp.bfloat16))
        acc[...] += jnp.dot(
            jnp.concatenate(lefts, axis=1), jnp.concatenate(rights, axis=0), preferred_element_type=jnp.float32
        )
        return carry

    lax.fori_loop(0, slots // GROUP, add_group, 0)
    second = lax.rem(lax.axis_index("sub"), 2) == 1
    for piece_at in range(pieces):
        at = slice(piece_at * rows, (piece_at + 1) * rows)
        real, imag = acc[at, 0:LANES], acc[at, LANES:2 * LANES]
        lanes = slice(piece_at * LANES, (piece_at + 1) * LANES)
        kept_ref[:, lanes] = jnp.where(second, imag, real)
        sent_ref[:, lanes] = jnp.where(second, real, imag)


def halves_of_image(pulses, offsets, geometry, counts):
    _, slots, _, samples = pulses.shape
    vmem = pl.BlockSpec(memory_space=pltpu.VMEM)
    hbm = pl.BlockSpec(memory_space=pltpu.HBM)
    held = (offsets, jnp.transpose(geometry, (1, 0, 2)), pulses)
    return pl.pallas_call(
        functools.partial(image_kernel, ROWS, COLS, BINS),
        out_shape=[jax.ShapeDtypeStruct((ROWS, COLS), jnp.float32)] * 2,
        in_specs=[pl.BlockSpec(memory_space=pltpu.SMEM), hbm, hbm, hbm],
        out_specs=[vmem, vmem],
        scratch_shapes=[
            pltpu.VMEM((slots, 2, samples), pulses.dtype),
            pltpu.VMEM((2, 2 * slots, LANES), jnp.float32),
            pltpu.VMEM((3, 1, slots), jnp.float32),
            pltpu.VMEM((1, slots), jnp.int32),
            pltpu.SMEM((1, slots), jnp.int32),
            pltpu.VMEM((LANES, LANES), jnp.float32),
            pltpu.VMEM((4, 8 * slots, LANES), jnp.float32),
            pltpu.VMEM((16, slots, LANES), jnp.float32),
            pltpu.VMEM((COLS // LANES * ROWS, 2 * LANES), jnp.float32),
            pltpu.SemaphoreType.DMA((4,)),
        ],
        compiler_params=pltpu.CompilerParams(vmem_limit_bytes=40 * 1024 * 1024),
    )(counts, *(pltpu.with_memory_space_constraint(x, pltpu.HBM) for x in held))


def shards(pulses, offsets, geometry, counts):
    members = lax.axis_size("sub")
    me = lax.axis_index("sub")
    kept, sent = halves_of_image(pulses, offsets, geometry, counts)

    def swap(value, distance):
        return lax.ppermute(value, "sub", [(i, i ^ distance) for i in range(members)])

    def ahead(value, distance):
        return lax.ppermute(value, "sub", [(i, i + distance) for i in range(members - distance)])

    odd = me % 2 == 1
    upper = me // 2 % 2 == 1
    block = me // 4
    blocks = members // 4
    got = swap(sent, 1)
    first = jnp.where(odd, got, kept)
    second = jnp.where(odd, kept, got)
    pair = first + second

    if blocks <= 4:
        nothing = jnp.zeros_like(pair)
        earlier = last = before_last = oldest = nothing
        for k in range(1, blocks):
            value = jnp.stack([pair, second]) if k == 2 else pair
            value = swap(value, 4 * k)
            if k == 2:
                oldest = jnp.where(block >= 2, value[1], nothing)
                value = value[0]
                before_last = jnp.where(block >= 2, value, nothing)
            source = block ^ k
            earlier = earlier + jnp.where(source < block, value, nothing)
            last = last + jnp.where(source == block - 1, value, nothing)
    else:
        last = ahead(pair, 4)
        before_last, oldest = ahead(jnp.stack([pair, second]), 8)
        earlier = last
        distance = 4
        while distance < members:
            earlier = earlier + ahead(earlier, distance)
            distance *= 2

    mine = jnp.stack([
        earlier + jnp.where(upper, 0.0, pair),
        last + jnp.where(upper, before_last, pair),
    ])
    other = swap(mine, 2)
    earlier = earlier + other[0]
    recent = last + other[1]
    frame_scale = 1.0 / math.sqrt(WINDOW)
    number = (me - me % 2 + 1).astype(jnp.float32)
    firsts = jnp.stack([(first + recent + oldest) * frame_scale, (earlier + first) / jnp.sqrt(number)])
    seconds = jnp.stack([(pair + recent) * frame_scale, (earlier + pair) / jnp.sqrt(number + 1.0)])

    own = jnp.where(odd, seconds, firsts)
    back = swap(jnp.where(odd, firsts, seconds), 1)
    real = jnp.where(odd, back, own)
    imag = jnp.where(odd, own, back)
    frames, cumulative = jnp.stack([real, imag], axis=1)
    return frames[None], cumulative[None]


def solution(mesh):
    return jax.shard_map(
        shards,
        mesh=mesh,
        in_specs=(
            P(("win", "sub"), None, None, None),
            P(("win", "sub"), None),
            P(("win", "sub"), None, None),
            P(("win", "sub")),
        ),
        out_specs=(P(("win", "sub"), None, None, None), P(("win", "sub"), None, None, None)),
        check_vma=False,
    )
```

```python
import functools
import math

import jax
import jax.numpy as jnp
from jax import lax
from jax.experimental import pallas as pl
from jax.experimental.pallas import tpu as pltpu
from jax.sharding import PartitionSpec as P

ROWS = 32
COLS = 512
BINS = 128
WINDOW = 8
LANES = 128

SIN = (3.141592580044369, -5.167706878903419, 2.5500313768938527, -0.5980451717629565, 0.07722012423151481)
COS = (0.999999953468687, -4.934792858755703, 4.0584119149345526, -1.3318801632613946, 0.21969679848706386)


def horner(coefficients, u):
    total = jnp.full_like(u, coefficients[-1])
    for c in coefficients[-2::-1]:
        total = total * u + c
    return total


def cis_turns(turns):
    f = turns - jnp.round(turns)
    u = f * f
    s = f * horner(SIN, u)
    c = horner(COS, u)
    return 1.0 - 2.0 * s * s, 2.0 * s * c


def cmul(a, b):
    return a[0] * b[0] - a[1] * b[1], a[0] * b[1] + a[1] * b[0]


def csquare(a):
    return a[0] * a[0] - a[1] * a[1], 2.0 * a[0] * a[1]


def image_kernel(rows, cols, width, counts_s, offsets_h, geometry_h, pulses_h, kept_ref, sent_ref,
                 held, window_f32, geometry_v, offsets_v, offsets_s, columns, seeds, steps, sems):
    slots, _, samples = held.shape
    pieces = cols // LANES
    half_x = rows // 2
    half_y = LANES // 2
    small = [
        pltpu.make_async_copy(source, target, sems.at[k])
        for k, (source, target) in enumerate((
            (geometry_h, geometry_v), (offsets_h, offsets_v), (offsets_h, offsets_s),
        ))
    ]
    for copy in small:
        copy.start()
    load = pltpu.make_async_copy(pulses_h.at[0], held, sems.at[3])
    load.start()

    b_index = lax.broadcasted_iota(jnp.int32, (width, width), 0).astype(jnp.float32)
    g_index = lax.broadcasted_iota(jnp.int32, (width, width), 1).astype(jnp.float32) - width // 2
    cosine, sine = cis_turns(b_index * g_index / width)
    fourier = jnp.concatenate(
        [jnp.concatenate([cosine, -sine], axis=1), jnp.concatenate([sine, cosine], axis=1)], axis=0
    )
    fourier_high = fourier.astype(jnp.bfloat16)
    fourier_low = (fourier - fourier_high.astype(jnp.float32)).astype(jnp.bfloat16)

    columns[...] = jnp.zeros_like(columns)
    for copy in small:
        copy.wait()
    for k in range(3):
        columns[k:k + 1, 0:slots] = geometry_v[k]
    columns[3:4, 0:slots] = offsets_v[...].astype(jnp.float32)
    by_pulse = jnp.transpose(columns[...])[0:slots]
    geo_centre = by_pulse[:, 0:1]
    slope_r = 0.05 * by_pulse[:, 1:2]
    slope_c = 0.05 * by_pulse[:, 2:3]
    offset = by_pulse[:, 3:4]
    shape = (slots, LANES)
    lane = lax.broadcasted_iota(jnp.int32, shape, 1).astype(jnp.float32)
    g = lane - width // 2
    theta = g / width + 0.37
    last_block = samples // LANES - 2
    block = jnp.minimum(jnp.floor(offset / LANES), last_block)
    rest = offset - LANES * block

    def sequence(first_seed, half):
        one = csquare(half)
        now = half
        for r in range(8):
            for k in range(2):
                seeds[first_seed + k, pl.ds(r, slots, stride=8), :] = now[k]
            if r < 7:
                now = cmul(now, one)
        return csquare(csquare(csquare(one)))

    def keep(first_step, value):
        for k in range(2):
            steps[first_step + k] = value[k]

    ratio = sequence(0, cis_turns((0.5 * slope_r) * theta))
    keep(0, ratio)
    ratio = sequence(2, cis_turns((0.5 * slope_c) * theta))
    for level in range(3):
        keep(2 + 2 * level, ratio)
        ratio = csquare(ratio)
    piece = csquare(ratio)

    phase = theta * (
        (width / 2.0 + width / 16.0 * geo_centre) - 0.5 * slope_r + slope_c * (half_y - 0.5 - cols // 2)
    )
    scaled = 37.0 * offset
    steps37 = (scaled - 100.0 * jnp.round(scaled / 100.0)) / 100.0
    circular = g * rest / width
    phase = phase + (circular - jnp.round(circular)) + steps37
    phase_cis = cis_turns(phase)

    load.wait()
    for p in range(slots):
        start = jnp.minimum(offsets_s[0, p] >> 7, last_block) * LANES
        pair = held[p, :, pl.ds(pl.multiple_of(start, LANES), 2 * LANES)].astype(jnp.float32)
        for half in range(2):
            window_f32[half, 2 * p:2 * p + 2, :] = pair[:, half * LANES:(half + 1) * LANES]
    in_first = lane >= rest
    parts = []
    for k in range(2):
        first = window_f32[0, pl.ds(k, slots, stride=2), :]
        second = window_f32[1, pl.ds(k, slots, stride=2), :]
        parts.append(jnp.where(in_first, first, second))
    folded = jnp.concatenate(parts, axis=1).astype(jnp.bfloat16)
    spectrum = jnp.dot(folded, fourier_high, preferred_element_type=jnp.float32) + jnp.dot(
        folded, fourier_low, preferred_element_type=jnp.float32
    )
    live = lax.broadcasted_iota(jnp.int32, shape, 0) < counts_s[0]
    scale = jnp.where(live, 1.0 / (width * math.sqrt(slots)), 0.0)
    now = cmul((spectrum[:, 0:LANES] * scale, spectrum[:, LANES:] * scale), phase_cis)
    for q in range(pieces):
        keep(8 + 2 * q, now)
        if q < pieces - 1:
            now = cmul(now, piece)

    lefts = []
    rights = []
    for pulse in range(slots):
        at = slice(8 * pulse, 8 * pulse + 8)

        def spread(k):
            return jnp.broadcast_to(steps[k, pulse:pulse + 1, :], (8, LANES))

        values = [(seeds[2, at, :], seeds[3, at, :])]
        for level in range(3):
            step_on = (spread(2 + 2 * level), spread(3 + 2 * level))
            values = values + [cmul(v, step_on) for v in values]
        rights.append(jnp.concatenate([v[k] for k in range(2) for v in values], axis=0).astype(jnp.bfloat16))
        values = [(seeds[0, at, :], seeds[1, at, :])]
        step_on = (spread(0), spread(1))
        while len(values) * 8 < half_x:
            values.append(cmul(values[-1], step_on))
        products = []
        for q in range(pieces):
            for t in range(2):
                factor = spread(8 + 2 * q + t)
                products += [factor * v[k] for k in range(2) for v in values]
        lefts.append(jnp.concatenate(products, axis=0).astype(jnp.bfloat16))
    acc = lax.dot_general(
        jnp.concatenate(lefts, axis=1), jnp.concatenate(rights, axis=1), (((1,), (1,)), ((), ())),
        preferred_element_type=jnp.float32,
    )

    lanes = lax.broadcasted_iota(jnp.int32, (8, LANES), 1)
    backward = LANES - 1 - lanes
    rolled_backward = lax.rem(backward + half_y, LANES)
    upside_down = 7 - lax.broadcasted_iota(jnp.int32, (8, LANES), 0)
    in_low = lanes < half_y
    is_second = lax.rem(lax.axis_index("sub"), 2) == 1
    for q in range(pieces):
        base = q * 4 * half_x
        for r in range(half_x // 8):
            ac, as_, bc, bs = (acc[base + n * half_x + 8 * r:base + n * half_x + 8 * r + 8, :] for n in range(4))
            for side in range(2):
                sign = 1.0 if side else -1.0
                both = []
                for real in range(2):
                    if real:
                        v = jnp.where(in_low, ac - sign * bs, -sign * as_ - bc)
                    else:
                        v = jnp.where(in_low, bc + sign * as_, ac - sign * bs)
                    ahead = v + pltpu.roll(v, half_y, 1)
                    behind = jnp.take_along_axis(v, rolled_backward, axis=1) - jnp.take_along_axis(v, backward, axis=1)
                    both.append(jnp.where(in_low, behind, ahead))
                if not side:
                    both = [jnp.take_along_axis(v, upside_down, axis=0) for v in both]
                imag, real = both
                row = half_x + 8 * r if side else half_x - 8 * (r + 1)
                at = (slice(row, row + 8), slice(q * LANES, (q + 1) * LANES))
                kept_ref[at] = jnp.where(is_second, imag, real)
                sent_ref[at] = jnp.where(is_second, real, imag)


def halves_of_image(pulses, offsets, geometry, counts):
    _, slots, _, samples = pulses.shape
    vmem = pl.BlockSpec(memory_space=pltpu.VMEM)
    hbm = pl.BlockSpec(memory_space=pltpu.HBM)
    held = (offsets, jnp.transpose(geometry, (1, 0, 2)), pulses)
    return pl.pallas_call(
        functools.partial(image_kernel, ROWS, COLS, BINS),
        out_shape=[jax.ShapeDtypeStruct((ROWS, COLS), jnp.float32)] * 2,
        in_specs=[pl.BlockSpec(memory_space=pltpu.SMEM), hbm, hbm, hbm],
        out_specs=[vmem, vmem],
        scratch_shapes=[
            pltpu.VMEM((slots, 2, samples), pulses.dtype),
            pltpu.VMEM((2, 2 * slots, LANES), jnp.float32),
            pltpu.VMEM((3, 1, slots), jnp.float32),
            pltpu.VMEM((1, slots), jnp.int32),
            pltpu.SMEM((1, slots), jnp.int32),
            pltpu.VMEM((LANES, LANES), jnp.float32),
            pltpu.VMEM((4, 8 * slots, LANES), jnp.float32),
            pltpu.VMEM((16, slots, LANES), jnp.float32),
            pltpu.SemaphoreType.DMA((4,)),
        ],
        compiler_params=pltpu.CompilerParams(vmem_limit_bytes=40 * 1024 * 1024),
    )(counts, *(pltpu.with_memory_space_constraint(x, pltpu.HBM) for x in held))


def shards(pulses, offsets, geometry, counts):
    members = lax.axis_size("sub")
    me = lax.axis_index("sub")
    kept, sent = halves_of_image(pulses, offsets, geometry, counts)

    def swap(value, distance):
        return lax.ppermute(value, "sub", [(i, i ^ distance) for i in range(members)])

    def ahead(value, distance):
        return lax.ppermute(value, "sub", [(i, i + distance) for i in range(members - distance)])

    odd = me % 2 == 1
    upper = me // 2 % 2 == 1
    block = me // 4
    blocks = members // 4
    got = swap(sent, 1)
    first = jnp.where(odd, got, kept)
    second = jnp.where(odd, kept, got)
    pair = first + second

    if blocks <= 4:
        nothing = jnp.zeros_like(pair)
        earlier = last = before_last = oldest = nothing
        for k in range(1, blocks):
            value = jnp.stack([pair, second]) if k == 2 else pair
            value = swap(value, 4 * k)
            if k == 2:
                oldest = jnp.where(block >= 2, value[1], nothing)
                value = value[0]
                before_last = jnp.where(block >= 2, value, nothing)
            source = block ^ k
            earlier = earlier + jnp.where(source < block, value, nothing)
            last = last + jnp.where(source == block - 1, value, nothing)
    else:
        last = ahead(pair, 4)
        before_last, oldest = ahead(jnp.stack([pair, second]), 8)
        earlier = last
        distance = 4
        while distance < members:
            earlier = earlier + ahead(earlier, distance)
            distance *= 2

    mine = jnp.stack([
        earlier + jnp.where(upper, 0.0, pair),
        last + jnp.where(upper, before_last, pair),
    ])
    other = swap(mine, 2)
    earlier = earlier + other[0]
    recent = last + other[1]
    frame_scale = 1.0 / math.sqrt(WINDOW)
    number = (me - me % 2 + 1).astype(jnp.float32)
    firsts = jnp.stack([(first + recent + oldest) * frame_scale, (earlier + first) / jnp.sqrt(number)])
    seconds = jnp.stack([(pair + recent) * frame_scale, (earlier + pair) / jnp.sqrt(number + 1.0)])

    own = jnp.where(odd, seconds, firsts)
    back = swap(jnp.where(odd, firsts, seconds), 1)
    real = jnp.where(odd, back, own)
    imag = jnp.where(odd, own, back)
    frames, cumulative = jnp.stack([real, imag], axis=1)
    return frames[None], cumulative[None]


def solution(mesh):
    return jax.shard_map(
        shards,
        mesh=mesh,
        in_specs=(
            P(("win", "sub"), None, None, None),
            P(("win", "sub"), None),
            P(("win", "sub"), None, None),
            P(("win", "sub")),
        ),
        out_specs=(P(("win", "sub"), None, None, None), P(("win", "sub"), None, None, None)),
        check_vma=False,
    )
```

```python
import functools
import math

import jax
import jax.numpy as jnp
from jax import lax
from jax.experimental import pallas as pl
from jax.experimental.pallas import tpu as pltpu
from jax.sharding import PartitionSpec as P

ROWS = 32
COLS = 512
BINS = 128
WINDOW = 8
LANES = 128

SIN = (3.141592580044369, -5.167706878903419, 2.5500313768938527, -0.5980451717629565, 0.07722012423151481)
COS = (0.999999953468687, -4.934792858755703, 4.0584119149345526, -1.3318801632613946, 0.21969679848706386)


def horner(coefficients, u):
    total = jnp.full_like(u, coefficients[-1])
    for c in coefficients[-2::-1]:
        total = total * u + c
    return total


def cis_turns(turns):
    f = turns - jnp.round(turns)
    u = f * f
    s = f * horner(SIN, u)
    c = horner(COS, u)
    return 1.0 - 2.0 * s * s, 2.0 * s * c


def cmul(a, b):
    return a[0] * b[0] - a[1] * b[1], a[0] * b[1] + a[1] * b[0]


def csquare(a):
    return a[0] * a[0] - a[1] * a[1], 2.0 * a[0] * a[1]


def image_kernel(rows, cols, width, counts_s, offsets_h, geometry_h, pulses_h, kept_ref, sent_ref,
                 held, window_f32, geometry_v, offsets_v, offsets_s, columns, seeds, steps, sems):
    slots, _, samples = held.shape
    pieces = cols // LANES
    half_x = rows // 2
    half_y = LANES // 2
    small = [
        pltpu.make_async_copy(source, target, sems.at[k])
        for k, (source, target) in enumerate((
            (geometry_h, geometry_v), (offsets_h, offsets_v), (offsets_h, offsets_s),
        ))
    ]
    for copy in small:
        copy.start()
    load = pltpu.make_async_copy(pulses_h.at[0], held, sems.at[3])
    load.start()

    b_index = lax.broadcasted_iota(jnp.int32, (width, width), 0).astype(jnp.float32)
    g_index = lax.broadcasted_iota(jnp.int32, (width, width), 1).astype(jnp.float32) - width // 2
    cosine, sine = cis_turns(b_index * g_index / width)
    fourier = jnp.concatenate(
        [jnp.concatenate([cosine, -sine], axis=1), jnp.concatenate([sine, cosine], axis=1)], axis=0
    )
    fourier_high = fourier.astype(jnp.bfloat16)
    fourier_low = (fourier - fourier_high.astype(jnp.float32)).astype(jnp.bfloat16)

    columns[...] = jnp.zeros_like(columns)
    for copy in small:
        copy.wait()
    for k in range(3):
        columns[k:k + 1, 0:slots] = geometry_v[k]
    columns[3:4, 0:slots] = offsets_v[...].astype(jnp.float32)
    by_pulse = jnp.transpose(columns[...])[0:slots]
    geo_centre = by_pulse[:, 0:1]
    slope_r = 0.05 * by_pulse[:, 1:2]
    slope_c = 0.05 * by_pulse[:, 2:3]
    offset = by_pulse[:, 3:4]
    shape = (slots, LANES)
    lane = lax.broadcasted_iota(jnp.int32, shape, 1).astype(jnp.float32)
    g = lane - width // 2
    theta = g / width + 0.37
    last_block = samples // LANES - 2
    block = jnp.minimum(jnp.floor(offset / LANES), last_block)
    rest = offset - LANES * block

    def sequence(first_seed, half):
        one = csquare(half)
        now = half
        for r in range(8):
            for k in range(2):
                seeds[first_seed + k, pl.ds(r, slots, stride=8), :] = now[k]
            if r < 7:
                now = cmul(now, one)
        return csquare(csquare(csquare(one)))

    def keep(first_step, value):
        for k in range(2):
            steps[first_step + k] = value[k]

    ratio = sequence(0, cis_turns((0.5 * slope_r) * theta))
    keep(0, ratio)
    ratio = sequence(2, cis_turns((0.5 * slope_c) * theta))
    for level in range(3):
        keep(2 + 2 * level, ratio)
        ratio = csquare(ratio)
    piece = csquare(ratio)

    phase = theta * (
        (width / 2.0 + width / 16.0 * geo_centre) - 0.5 * slope_r + slope_c * (half_y - 0.5 - cols // 2)
    )
    scaled = 37.0 * offset
    steps37 = (scaled - 100.0 * jnp.round(scaled / 100.0)) / 100.0
    circular = g * rest / width
    phase = phase + (circular - jnp.round(circular)) + steps37
    phase_cis = cis_turns(phase)

    load.wait()
    for p in range(slots):
        start = jnp.minimum(offsets_s[0, p] >> 7, last_block) * LANES
        pair = held[p, :, pl.ds(pl.multiple_of(start, LANES), 2 * LANES)].astype(jnp.float32)
        for half in range(2):
            window_f32[half, 2 * p:2 * p + 2, :] = pair[:, half * LANES:(half + 1) * LANES]
    in_first = lane >= rest
    parts = []
    for k in range(2):
        first = window_f32[0, pl.ds(k, slots, stride=2), :]
        second = window_f32[1, pl.ds(k, slots, stride=2), :]
        parts.append(jnp.where(in_first, first, second))
    folded = jnp.concatenate(parts, axis=1).astype(jnp.bfloat16)
    spectrum = jnp.dot(folded, fourier_high, preferred_element_type=jnp.float32) + jnp.dot(
        folded, fourier_low, preferred_element_type=jnp.float32
    )
    live = lax.broadcasted_iota(jnp.int32, shape, 0) < counts_s[0]
    scale = jnp.where(live, 1.0 / (width * math.sqrt(slots)), 0.0)
    now = cmul((spectrum[:, 0:LANES] * scale, spectrum[:, LANES:] * scale), phase_cis)
    for q in range(pieces):
        keep(8 + 2 * q, now)
        if q < pieces - 1:
            now = cmul(now, piece)

    lefts = []
    rights = []
    for pulse in range(slots):
        at = slice(8 * pulse, 8 * pulse + 8)

        def spread(k):
            return jnp.broadcast_to(steps[k, pulse:pulse + 1, :], (8, LANES))

        values = [(seeds[2, at, :], seeds[3, at, :])]
        for level in range(3):
            step_on = (spread(2 + 2 * level), spread(3 + 2 * level))
            values = values + [cmul(v, step_on) for v in values]
        rights.append(jnp.concatenate([v[k] for k in range(2) for v in values], axis=0).astype(jnp.bfloat16))
        values = [(seeds[0, at, :], seeds[1, at, :])]
        step_on = (spread(0), spread(1))
        while len(values) * 8 < half_x:
            values.append(cmul(values[-1], step_on))
        products = []
        for q in range(pieces):
            for t in range(2):
                factor = spread(8 + 2 * q + t)
                products += [factor * v[k] for k in range(2) for v in values]
        lefts.append(jnp.concatenate(products, axis=0).astype(jnp.bfloat16))
    acc = lax.dot_general(
        jnp.concatenate(lefts, axis=1), jnp.concatenate(rights, axis=1), (((1,), (1,)), ((), ())),
        preferred_element_type=jnp.float32,
    )

    lanes = lax.broadcasted_iota(jnp.int32, (8, LANES), 1)
    backward = LANES - 1 - lanes
    rolled_backward = lax.rem(backward + half_y, LANES)
    upside_down = 7 - lax.broadcasted_iota(jnp.int32, (8, LANES), 0)
    in_low = lanes < half_y
    is_second = lax.rem(lax.axis_index("sub"), 2) == 1
    for q in range(pieces):
        base = q * 4 * half_x
        for r in range(half_x // 8):
            ac, as_, bc, bs = (acc[base + n * half_x + 8 * r:base + n * half_x + 8 * r + 8, :] for n in range(4))
            for side in range(2):
                sign = 1.0 if side else -1.0
                both = []
                for real in range(2):
                    if real:
                        v = jnp.where(in_low, ac - sign * bs, -sign * as_ - bc)
                    else:
                        v = jnp.where(in_low, bc + sign * as_, ac - sign * bs)
                    ahead = v + pltpu.roll(v, half_y, 1)
                    behind = jnp.take_along_axis(v, rolled_backward, axis=1) - jnp.take_along_axis(v, backward, axis=1)
                    both.append(jnp.where(in_low, behind, ahead))
                if not side:
                    both = [jnp.take_along_axis(v, upside_down, axis=0) for v in both]
                imag, real = both
                row = half_x + 8 * r if side else half_x - 8 * (r + 1)
                at = (slice(row, row + 8), slice(q * LANES, (q + 1) * LANES))
                kept_ref[at] = jnp.where(is_second, imag, real)
                sent_ref[at] = jnp.where(is_second, real, imag)


def halves_of_image(pulses, offsets, geometry, counts):
    _, slots, _, samples = pulses.shape
    vmem = pl.BlockSpec(memory_space=pltpu.VMEM)
    hbm = pl.BlockSpec(memory_space=pltpu.HBM)
    held = (offsets, jnp.transpose(geometry, (1, 0, 2)), pulses)
    return pl.pallas_call(
        functools.partial(image_kernel, ROWS, COLS, BINS),
        out_shape=[jax.ShapeDtypeStruct((ROWS, COLS), jnp.float32)] * 2,
        in_specs=[pl.BlockSpec(memory_space=pltpu.SMEM), hbm, hbm, hbm],
        out_specs=[vmem, vmem],
        scratch_shapes=[
            pltpu.VMEM((slots, 2, samples), pulses.dtype),
            pltpu.VMEM((2, 2 * slots, LANES), jnp.float32),
            pltpu.VMEM((3, 1, slots), jnp.float32),
            pltpu.VMEM((1, slots), jnp.int32),
            pltpu.SMEM((1, slots), jnp.int32),
            pltpu.VMEM((LANES, LANES), jnp.float32),
            pltpu.VMEM((4, 8 * slots, LANES), jnp.float32),
            pltpu.VMEM((16, slots, LANES), jnp.float32),
            pltpu.SemaphoreType.DMA((4,)),
        ],
        compiler_params=pltpu.CompilerParams(vmem_limit_bytes=40 * 1024 * 1024),
    )(counts, *(pltpu.with_memory_space_constraint(x, pltpu.HBM) for x in held))


def shards(pulses, offsets, geometry, counts):
    members = lax.axis_size("sub")
    me = lax.axis_index("sub")
    kept, sent = halves_of_image(pulses, offsets, geometry, counts)

    def swap(value, distance):
        return lax.ppermute(value, "sub", [(i, i ^ distance) for i in range(members)])

    def ahead(value, distance):
        return lax.ppermute(value, "sub", [(i, i + distance) for i in range(members - distance)])

    odd = me % 2 == 1
    upper = me // 2 % 2 == 1
    block = me // 4
    blocks = members // 4
    reach = WINDOW - 1
    links = [(i, i + reach) for i in range(1, members - reach, 2)]
    whole = jnp.where(odd, jnp.stack([sent, kept]), 0.0)
    oldest = lax.ppermute(whole, "sub", links)
    got = swap(sent, 1)
    first = jnp.where(odd, got, kept)
    second = jnp.where(odd, kept, got)
    pair = first + second

    if blocks <= 4:
        nothing = jnp.zeros_like(pair)
        earlier = last = before_last = nothing
        for k in range(blocks - 1, 0, -1):
            if k == 2:
                value = before_last = ahead(pair, 8)
            else:
                value = swap(pair, 4 * k)
            source = block ^ k
            earlier = earlier + jnp.where(source < block, value, nothing)
            last = last + jnp.where(source == block - 1, value, nothing)
    else:
        last = ahead(pair, 4)
        before_last = ahead(pair, 8)
        earlier = last
        distance = 4
        while distance < members:
            earlier = earlier + ahead(earlier, distance)
            distance *= 2

    mine = jnp.stack([
        earlier + jnp.where(upper, 0.0, pair),
        last + jnp.where(upper, before_last, pair),
    ])
    other = swap(mine, 2)
    other, oldest = lax.optimization_barrier((other, oldest))
    earlier = earlier + other[0]
    recent = last + other[1]
    frame_scale = 1.0 / math.sqrt(WINDOW)
    number = (me - me % 2 + 1).astype(jnp.float32)
    firsts = jnp.stack([(first + recent) * frame_scale, (earlier + first) / jnp.sqrt(number)])
    seconds = jnp.stack([(pair + recent) * frame_scale, (earlier + pair) / jnp.sqrt(number + 1.0)])

    own = jnp.where(odd, seconds, firsts)
    back = swap(jnp.where(odd, firsts, seconds), 1)
    real = jnp.where(odd, back, own)
    imag = jnp.where(odd, own, back)
    frames = jnp.stack([real[0] + oldest[0] * frame_scale, imag[0] + oldest[1] * frame_scale])
    cumulative = jnp.stack([real[1], imag[1]])
    return frames[None], cumulative[None]


def solution(mesh):
    return jax.shard_map(
        shards,
        mesh=mesh,
        in_specs=(
            P(("win", "sub"), None, None, None),
            P(("win", "sub"), None),
            P(("win", "sub"), None, None),
            P(("win", "sub")),
        ),
        out_specs=(P(("win", "sub"), None, None, None), P(("win", "sub"), None, None, None)),
        check_vma=False,
    )
```

```python
import functools
import math

import jax
import jax.numpy as jnp
from jax import lax
from jax.experimental import pallas as pl
from jax.experimental.pallas import tpu as pltpu
from jax.sharding import PartitionSpec as P

ROWS = 32
COLS = 512
BINS = 128
WINDOW = 8
LANES = 128

SIN = (3.141592580044369, -5.167706878903419, 2.5500313768938527, -0.5980451717629565, 0.07722012423151481)
COS = (0.999999953468687, -4.934792858755703, 4.0584119149345526, -1.3318801632613946, 0.21969679848706386)


def horner(coefficients, u):
    total = jnp.full_like(u, coefficients[-1])
    for c in coefficients[-2::-1]:
        total = total * u + c
    return total


def cis_turns(turns):
    f = turns - jnp.round(turns)
    u = f * f
    s = f * horner(SIN, u)
    c = horner(COS, u)
    return 1.0 - 2.0 * s * s, 2.0 * s * c


def cmul(a, b):
    return a[0] * b[0] - a[1] * b[1], a[0] * b[1] + a[1] * b[0]


def csquare(a):
    return a[0] * a[0] - a[1] * a[1], 2.0 * a[0] * a[1]


def image_kernel(rows, cols, width, counts_s, offsets_h, geometry_h, pulses_h, kept_ref, sent_ref,
                 held, window_f32, geometry_v, offsets_v, offsets_s, columns, seeds, steps, sems):
    slots, _, samples = held.shape
    pieces = cols // LANES
    half_x = rows // 2
    half_y = LANES // 2
    small = [
        pltpu.make_async_copy(source, target, sems.at[k])
        for k, (source, target) in enumerate((
            (geometry_h, geometry_v), (offsets_h, offsets_v), (offsets_h, offsets_s),
        ))
    ]
    for copy in small:
        copy.start()
    load = pltpu.make_async_copy(pulses_h.at[0], held, sems.at[3])
    load.start()

    columns[...] = jnp.zeros_like(columns)
    for copy in small[:2]:
        copy.wait()
    for k in range(3):
        columns[k:k + 1, 0:slots] = geometry_v[k]
    columns[3:4, 0:slots] = offsets_v[...].astype(jnp.float32)
    by_pulse = jnp.transpose(columns[...])[0:slots]
    geo_centre = by_pulse[:, 0:1]
    slope_r = 0.05 * by_pulse[:, 1:2]
    slope_c = 0.05 * by_pulse[:, 2:3]
    offset = by_pulse[:, 3:4]
    shape = (slots, LANES)
    lane = lax.broadcasted_iota(jnp.int32, shape, 1).astype(jnp.float32)
    g = lane - width // 2
    theta = g / width + 0.37
    last_block = samples // LANES - 2
    block = jnp.minimum(jnp.floor(offset / LANES), last_block)
    rest = offset - LANES * block

    def sequence(first_seed, half):
        one = csquare(half)
        now = half
        for r in range(8):
            for k in range(2):
                seeds[first_seed + k, pl.ds(r, slots, stride=8), :] = now[k]
            if r < 7:
                now = cmul(now, one)
        return csquare(csquare(csquare(one)))

    def keep(first_step, value):
        for k in range(2):
            steps[first_step + k] = value[k]

    ratio = sequence(0, cis_turns((0.5 * slope_r) * theta))
    keep(0, ratio)
    ratio = sequence(2, cis_turns((0.5 * slope_c) * theta))
    for level in range(3):
        keep(2 + 2 * level, ratio)
        ratio = csquare(ratio)
    piece = csquare(ratio)

    phase = theta * (
        (width / 2.0 + width / 16.0 * geo_centre) - 0.5 * slope_r + slope_c * (half_y - 0.5 - cols // 2)
    )
    scaled = 37.0 * offset
    steps37 = (scaled - 100.0 * jnp.round(scaled / 100.0)) / 100.0
    circular = g * rest / width
    phase = phase + (circular - jnp.round(circular)) + steps37
    phase_cis = cis_turns(phase)

    b_index = lax.broadcasted_iota(jnp.int32, (width, width), 0).astype(jnp.float32)
    g_index = lax.broadcasted_iota(jnp.int32, (width, width), 1).astype(jnp.float32) - width // 2
    cosine, sine = cis_turns(b_index * g_index / width)
    fourier = jnp.concatenate(
        [jnp.concatenate([cosine, -sine], axis=1), jnp.concatenate([sine, cosine], axis=1)], axis=0
    )
    fourier_high = fourier.astype(jnp.bfloat16)
    fourier_low = (fourier - fourier_high.astype(jnp.float32)).astype(jnp.bfloat16)

    small[2].wait()
    load.wait()
    for p in range(slots):
        start = jnp.minimum(offsets_s[0, p] >> 7, last_block) * LANES
        pair = held[p, :, pl.ds(pl.multiple_of(start, LANES), 2 * LANES)].astype(jnp.float32)
        for half in range(2):
            window_f32[half, 2 * p:2 * p + 2, :] = pair[:, half * LANES:(half + 1) * LANES]
    in_first = lane >= rest
    parts = []
    for k in range(2):
        first = window_f32[0, pl.ds(k, slots, stride=2), :]
        second = window_f32[1, pl.ds(k, slots, stride=2), :]
        parts.append(jnp.where(in_first, first, second))
    folded = jnp.concatenate(parts, axis=1).astype(jnp.bfloat16)
    spectrum = jnp.dot(folded, fourier_high, preferred_element_type=jnp.float32) + jnp.dot(
        folded, fourier_low, preferred_element_type=jnp.float32
    )
    live = lax.broadcasted_iota(jnp.int32, shape, 0) < counts_s[0]
    scale = jnp.where(live, 1.0 / (width * math.sqrt(slots)), 0.0)
    now = cmul((spectrum[:, 0:LANES] * scale, spectrum[:, LANES:] * scale), phase_cis)
    for q in range(pieces):
        keep(8 + 2 * q, now)
        if q < pieces - 1:
            now = cmul(now, piece)

    lefts = []
    rights = []
    for pulse in range(slots):
        at = slice(8 * pulse, 8 * pulse + 8)

        def spread(k):
            return jnp.broadcast_to(steps[k, pulse:pulse + 1, :], (8, LANES))

        values = [(seeds[2, at, :], seeds[3, at, :])]
        for level in range(3):
            step_on = (spread(2 + 2 * level), spread(3 + 2 * level))
            values = values + [cmul(v, step_on) for v in values]
        rights.append(jnp.concatenate([v[k] for k in range(2) for v in values], axis=0).astype(jnp.bfloat16))
        values = [(seeds[0, at, :], seeds[1, at, :])]
        step_on = (spread(0), spread(1))
        while len(values) * 8 < half_x:
            values.append(cmul(values[-1], step_on))
        products = []
        for q in range(pieces):
            for t in range(2):
                factor = spread(8 + 2 * q + t)
                products += [factor * v[k] for k in range(2) for v in values]
        lefts.append(jnp.concatenate(products, axis=0).astype(jnp.bfloat16))
    acc = lax.dot_general(
        jnp.concatenate(lefts, axis=1), jnp.concatenate(rights, axis=1), (((1,), (1,)), ((), ())),
        preferred_element_type=jnp.float32,
    )

    lanes = lax.broadcasted_iota(jnp.int32, (8, LANES), 1)
    backward = LANES - 1 - lanes
    rolled_backward = lax.rem(backward + half_y, LANES)
    upside_down = 7 - lax.broadcasted_iota(jnp.int32, (8, LANES), 0)
    in_low = lanes < half_y
    is_second = lax.rem(lax.axis_index("sub"), 2) == 1
    for q in range(pieces):
        base = q * 4 * half_x
        for r in range(half_x // 8):
            ac, as_, bc, bs = (acc[base + n * half_x + 8 * r:base + n * half_x + 8 * r + 8, :] for n in range(4))
            for side in range(2):
                sign = 1.0 if side else -1.0
                both = []
                for real in range(2):
                    if real:
                        v = jnp.where(in_low, ac - sign * bs, -sign * as_ - bc)
                    else:
                        v = jnp.where(in_low, bc + sign * as_, ac - sign * bs)
                    ahead = v + pltpu.roll(v, half_y, 1)
                    behind = jnp.take_along_axis(v, rolled_backward, axis=1) - jnp.take_along_axis(v, backward, axis=1)
                    both.append(jnp.where(in_low, behind, ahead))
                if not side:
                    both = [jnp.take_along_axis(v, upside_down, axis=0) for v in both]
                imag, real = both
                row = half_x + 8 * r if side else half_x - 8 * (r + 1)
                at = (slice(row, row + 8), slice(q * LANES, (q + 1) * LANES))
                kept_ref[at] = jnp.where(is_second, imag, real)
                sent_ref[at] = jnp.where(is_second, real, imag)


def halves_of_image(pulses, offsets, geometry, counts):
    _, slots, _, samples = pulses.shape
    vmem = pl.BlockSpec(memory_space=pltpu.VMEM)
    hbm = pl.BlockSpec(memory_space=pltpu.HBM)
    held = (offsets, jnp.transpose(geometry, (1, 0, 2)), pulses)
    return pl.pallas_call(
        functools.partial(image_kernel, ROWS, COLS, BINS),
        out_shape=[jax.ShapeDtypeStruct((ROWS, COLS), jnp.float32)] * 2,
        in_specs=[pl.BlockSpec(memory_space=pltpu.SMEM), hbm, hbm, hbm],
        out_specs=[vmem, vmem],
        scratch_shapes=[
            pltpu.VMEM((slots, 2, samples), pulses.dtype),
            pltpu.VMEM((2, 2 * slots, LANES), jnp.float32),
            pltpu.VMEM((3, 1, slots), jnp.float32),
            pltpu.VMEM((1, slots), jnp.int32),
            pltpu.SMEM((1, slots), jnp.int32),
            pltpu.VMEM((LANES, LANES), jnp.float32),
            pltpu.VMEM((4, 8 * slots, LANES), jnp.float32),
            pltpu.VMEM((16, slots, LANES), jnp.float32),
            pltpu.SemaphoreType.DMA((4,)),
        ],
        compiler_params=pltpu.CompilerParams(vmem_limit_bytes=40 * 1024 * 1024),
    )(counts, *(pltpu.with_memory_space_constraint(x, pltpu.HBM) for x in held))


def shards(pulses, offsets, geometry, counts):
    members = lax.axis_size("sub")
    me = lax.axis_index("sub")
    kept, sent = halves_of_image(pulses, offsets, geometry, counts)

    def swap(value, distance):
        return lax.ppermute(value, "sub", [(i, i ^ distance) for i in range(members)])

    def ahead(value, distance):
        return lax.ppermute(value, "sub", [(i, i + distance) for i in range(members - distance)])

    odd = me % 2 == 1
    upper = me // 2 % 2 == 1
    block = me // 4
    blocks = members // 4
    reach = WINDOW - 1
    links = [(i, i + reach) for i in range(1, members - reach, 2)]
    whole = jnp.where(odd, jnp.stack([sent, kept]), 0.0)
    oldest = lax.ppermute(whole, "sub", links)
    got = swap(sent, 1)
    first = jnp.where(odd, got, kept)
    second = jnp.where(odd, kept, got)
    pair = first + second

    if blocks <= 4:
        nothing = jnp.zeros_like(pair)
        earlier = last = before_last = nothing
        for k in range(blocks - 1, 0, -1):
            if k == 2:
                value = before_last = ahead(pair, 8)
            else:
                value = swap(pair, 4 * k)
            source = block ^ k
            earlier = earlier + jnp.where(source < block, value, nothing)
            last = last + jnp.where(source == block - 1, value, nothing)
    else:
        last = ahead(pair, 4)
        before_last = ahead(pair, 8)
        earlier = last
        distance = 4
        while distance < members:
            earlier = earlier + ahead(earlier, distance)
            distance *= 2

    mine = jnp.stack([
        earlier + jnp.where(upper, 0.0, pair),
        last + jnp.where(upper, before_last, pair),
    ])
    other = swap(mine, 2)
    other, oldest = lax.optimization_barrier((other, oldest))
    earlier = earlier + other[0]
    recent = last + other[1]
    frame_scale = 1.0 / math.sqrt(WINDOW)
    number = (me - me % 2 + 1).astype(jnp.float32)
    firsts = jnp.stack([(first + recent) * frame_scale, (earlier + first) / jnp.sqrt(number)])
    seconds = jnp.stack([(pair + recent) * frame_scale, (earlier + pair) / jnp.sqrt(number + 1.0)])

    own = jnp.where(odd, seconds, firsts)
    back = swap(jnp.where(odd, firsts, seconds), 1)
    real = jnp.where(odd, back, own)
    imag = jnp.where(odd, own, back)
    frames = jnp.stack([real[0] + oldest[0] * frame_scale, imag[0] + oldest[1] * frame_scale])
    cumulative = jnp.stack([real[1], imag[1]])
    return frames[None], cumulative[None]


def solution(mesh):
    return jax.shard_map(
        shards,
        mesh=mesh,
        in_specs=(
            P(("win", "sub"), None, None, None),
            P(("win", "sub"), None),
            P(("win", "sub"), None, None),
            P(("win", "sub")),
        ),
        out_specs=(P(("win", "sub"), None, None, None), P(("win", "sub"), None, None, None)),
        check_vma=False,
    )
```
